32 devices in a mesh: grp: 2 (over x), lat: 16 (over z, y, core).
Axes of the slice: x: 2, y: 2, z: 4, core: 2. Of those that a mesh axis runs over, the one named last changes fastest.
Arguments:
- features: bfloat16 [2, 32, 192, 512], P('grp', 'lat'), parts along dimension 0, may hold values from -120 to 120
- noise_index: int32 [2], P('grp'), parts along dimension 0, may hold values from 0 to 17
- sigma_table: float32 [18], replicated, may hold values from 0.002 to 80
- affine_weight: bfloat16 [128, 1024], replicated, may hold values from -0.5 to 0.5
- norm_gain: float32 [3, 512], replicated, may hold values from 0.1 to 1.9
- norm_bias: float32 [3, 512], replicated, may hold values from -3 to 3
- conv1_weight: bfloat16 [3, 3, 512, 512], replicated, may hold values from -0.09375 to 0.09375
- conv2_weight: bfloat16 [3, 3, 512, 512], replicated, may hold values from -0.09375 to 0.09375
- conv_bias: float32 [2, 512], replicated, may hold values from -3 to 3
- qkv_weight: bfloat16 [512, 1536], replicated, may hold values from -3 to 3
- proj_weight: bfloat16 [512, 512], replicated, may hold values from -0.25 to 0.25
- proj_bias: float32 [512], replicated, may hold values from -3 to 3
Outputs:
- bottleneck: bfloat16 [2, 16, 96, 512], P('grp', 'lat'), parts along dimension 0
The draws below stay inside these ranges and needn't reach their ends.
There are 2 independent parts, one for each index of `grp`. The reference program is written for one: setup_inputs(seed, part) draws one part's arguments, and reference() takes and returns one part's arrays. A program takes and returns all parts, laid end to end along the dimension named above; an argument that names none is the same for every part. Nothing has to cross between parts.
All inputs are finite; a program needn't handle non-finite values.
Results may differ from the reference program's by a relative error of at most 0.012.
The reference program's roundings to bfloat16 on the way (of `fourier`, `active`, `middle`, `level_one`, `normed`, `projected`, `weights` and `attended`) count: a program that leaves them out, or rounds other values in their place, can miss the bound.
Values may be sent and summed in bfloat16 or wider, within the bound.
A program may use at most 128 MiB of HBM per device.

```python
import math
import jax
import jax.numpy as jnp
from jax import lax

C = 512
HEAD_DIM = 64
GROUPS = 32
FREQS = 64
LEVELS = 18
MEMBERS = 1
W1 = 192
H1 = 32


def draw_features(key, part):
    base_key, chan_key, rough_key, row_key = jax.random.split(key, 4)
    full_shape = (MEMBERS, H1, W1, C)
    row_factor = jnp.exp(jax.random.uniform(row_key, (H1,), jnp.float32, 0.0, jnp.log(10.0)))
    channel_scale = jnp.exp(jax.random.uniform(chan_key, (C,), jnp.float32, 0.0, jnp.log(10.0)))
    roughness = jnp.exp(jax.random.uniform(rough_key, (1, H1, W1, 1), jnp.float32, 0.0, jnp.log(2.0)))
    samples = jnp.clip(jax.random.normal(base_key, full_shape, jnp.float32), -6.0, 6.0)
    values = samples * row_factor[None, :, None, None] * channel_scale * roughness / 10.0
    return values.astype(jnp.bfloat16)


def draw_qkv_weight(key, part):
    own_key = jax.random.fold_in(key, 0)
    own_part = jnp.clip(jax.random.normal(own_key, (C, 3 * C), jnp.float32), -6.0, 6.0)
    factor = jnp.concatenate([jnp.full((1, 2 * C), 1.7, jnp.float32), jnp.ones((1, C), jnp.float32)], axis=1)
    table = own_part * factor / C ** 0.5
    return table.astype(jnp.bfloat16)


def gaussian(key, extent, width, most, held_as=jnp.bfloat16):
    array = width * jax.random.normal(key, extent, jnp.float32)
    return jnp.clip(array, min=-most, max=most).astype(held_as)


def setup_inputs(seed: int = 0, part: int = 0) -> dict:
    key_list = jax.random.split(jax.random.key(seed), 13)
    part_keys = jax.random.split(jax.random.fold_in(key_list[12], part), 13)
    return {
        "features": draw_features(jax.random.fold_in(jax.random.fold_in(key_list[12], part), 71), part),
        "noise_index": jax.random.randint(part_keys[1], (MEMBERS,), 0, LEVELS).astype(jnp.int32),
        "sigma_table": jnp.clip(jnp.exp(jax.random.uniform(key_list[2], (LEVELS,), jnp.float32, math.log(0.002), math.log(80.0))), 0.002, 80.0),
        "affine_weight": gaussian(key_list[3], (2 * FREQS, 2 * C), (2 * FREQS) ** -0.5, 0.5),
        "norm_gain": jnp.clip(1.0 + 0.18 * jax.random.normal(key_list[4], (3, C), jnp.float32), 0.1, 1.9),
        "norm_bias": gaussian(key_list[5], (3, C), 0.5, 3.0, jnp.float32),
        "conv1_weight": gaussian(key_list[6], (3, 3, C, C), (9 * C) ** -0.5, 0.09375),
        "conv2_weight": gaussian(key_list[7], (3, 3, C, C), (9 * C) ** -0.5, 0.09375),
        "conv_bias": gaussian(key_list[8], (2, C), 0.5, 3.0, jnp.float32),
        "qkv_weight": draw_qkv_weight(jax.random.fold_in(key_list[12], 71), part),
        "proj_weight": gaussian(key_list[10], (C, C), C ** -0.5, 0.25),
        "proj_bias": gaussian(key_list[11], (C,), 0.5, 3.0, jnp.float32),
    }


eps = 1e-05
skip_gain = 0.7071067811865476

def noise_terms(noise_index, sigma_table, affine_weight):
    levels_count = sigma_table.shape[0]
    chosen = (noise_index[:, None] == jnp.arange(levels_count, dtype=jnp.int32)[None, :]).astype(jnp.float32)
    sigmas = lax.optimization_barrier(jnp.sum(chosen * sigma_table[None, :], axis=1))
    log_level = jnp.log(sigmas) / 4.0
    frequency = jnp.exp(-math.log(10000.0) * jnp.arange(FREQS, dtype=jnp.float32) / FREQS)
    angles = log_level[:, None] * frequency[None, :]
    fourier = jnp.concatenate([jnp.cos(angles), jnp.sin(angles)], axis=1).astype(jnp.bfloat16)
    affine = jnp.dot(fourier, affine_weight, preferred_element_type=jnp.float32)
    channels = affine.shape[1] // 2
    return (affine[:, :channels], affine[:, channels:])

def group_norm(values, norm_scale, norm_offset):
    members, height, breadth, channels = values.shape
    grouped = values.reshape(members, height * breadth, GROUPS, channels // GROUPS)
    center = lax.optimization_barrier(jnp.mean(grouped, axis=(1, 3), keepdims=True))
    spread = lax.optimization_barrier(jnp.mean(jnp.square(grouped - center), axis=(1, 3), keepdims=True))
    normed = (grouped - center) * lax.rsqrt(spread + eps)
    return normed.reshape(values.shape) * norm_scale + norm_offset

def convolve(values, kernel):
    return lax.conv_general_dilated(values.astype(jnp.float32), kernel.astype(jnp.float32), (1, 1), ((1, 1), (1, 1)), dimension_numbers=('NHWC', 'HWIO', 'NHWC'), precision=lax.Precision.HIGHEST)

def attend(query_rows, key_rows, value_rows):
    tokens = query_rows.shape[0]
    blocking = math.gcd(tokens, 512)
    key_full = key_rows.astype(jnp.float32)
    value_full = value_rows.astype(jnp.float32)

    def score_block(query_block):
        scores = jnp.einsum('qhd,khd->qhk', query_block.astype(jnp.float32), key_full, precision=lax.Precision.HIGHEST) * HEAD_DIM ** (-0.5)
        largest = lax.optimization_barrier(jnp.max(scores, axis=-1, keepdims=True))
        weights = jnp.exp(scores - largest)
        totals = lax.optimization_barrier(jnp.sum(weights, axis=-1))
        rounded = lax.optimization_barrier(weights.astype(jnp.bfloat16)).astype(jnp.float32)
        blended = jnp.einsum('qhk,khd->qhd', rounded, value_full, precision=lax.Precision.HIGHEST)
        return blended / totals[..., None]
    blocks = query_rows.reshape(tokens // blocking, blocking, query_rows.shape[1], query_rows.shape[2])
    return lax.map(score_block, blocks).reshape(tokens, -1)

def reference(features, noise_index, sigma_table, affine_weight, norm_gain, norm_bias, conv1_weight, conv2_weight, conv_bias, qkv_weight, proj_weight, proj_bias):
    film_scale, film_shift = noise_terms(noise_index, sigma_table, affine_weight)
    film_scale = film_scale[:, None, None, :]
    film_shift = film_shift[:, None, None, :]
    source = features.astype(jnp.float32)
    active = jax.nn.silu(group_norm(source, norm_gain[0], norm_bias[0])).astype(jnp.bfloat16)
    first_conv = convolve(active, conv1_weight) + conv_bias[0]
    middle = jax.nn.silu(group_norm(first_conv, norm_gain[1], norm_bias[1]) * (1.0 + film_scale) + film_shift).astype(jnp.bfloat16)
    second_conv = convolve(middle, conv2_weight) + conv_bias[1]
    level_one = ((source + second_conv) * skip_gain).astype(jnp.bfloat16)
    level_one = lax.optimization_barrier(level_one)
    members, height, breadth, channels = level_one.shape
    pooled = lax.optimization_barrier(jnp.mean(level_one.astype(jnp.float32).reshape(members, height // 2, 2, breadth // 2, 2, channels), axis=(2, 4)))
    normed = group_norm(pooled, norm_gain[2], norm_bias[2]).astype(jnp.bfloat16)
    tokens = height // 2 * (breadth // 2)
    head_count = channels // HEAD_DIM
    projected = jnp.dot(normed.reshape(members * tokens, channels), qkv_weight, preferred_element_type=jnp.float32).astype(jnp.bfloat16)
    projected = projected.reshape(members, tokens, 3, head_count, HEAD_DIM)
    attended_list = [attend(projected[member, :, 0], projected[member, :, 1], projected[member, :, 2]) for member in range(members)]
    attended = jnp.stack(attended_list).reshape(members * tokens, channels).astype(jnp.bfloat16)
    output_proj = jnp.dot(attended, proj_weight, preferred_element_type=jnp.float32) + proj_bias
    return ((pooled + output_proj.reshape(pooled.shape)) * skip_gain).astype(jnp.bfloat16)
```

```python
import math

import jax
import jax.numpy as jnp
from jax import lax
from jax.experimental import pallas as pl
from jax.experimental.pallas import tpu as pltpu
from jax.sharding import PartitionSpec as P

HEAD_DIM = 64
GROUPS = 32
FREQS = 64
LANES = 128

eps = 1e-05
skip_gain = 0.7071067811865476


def group_totals(sums, group_width):
    lane = lax.broadcasted_iota(jnp.int32, sums.shape, 1)
    step = 1
    while step < group_width:
        ahead = pltpu.roll(sums, LANES - step, 1)
        behind = pltpu.roll(sums, step, 1)
        sums = sums + jnp.where((lane // step) % 2 == 0, ahead, behind)
        step *= 2
    return sums


def silu(values):
    return values / (1.0 + jnp.exp(-values))


def kernel(
    n,
    noise_ref,
    sigma_ref,
    features_ref,
    affine_hbm,
    gain_ref,
    bias_ref,
    conv1_hbm,
    conv2_hbm,
    conv_bias_ref,
    qkv_hbm,
    proj_hbm,
    proj_bias_ref,
    out_ref,
    affine,
    w1,
    w2,
    wqkv,
    wproj,
    abuf,
    first,
    edges,
    halo1,
    halo2,
    stats,
    gath,
    pooled_ref,
    qm,
    top,
    total,
    acc,
    w_sem,
    stat_send,
    stat_recv,
    halo_send,
    halo_recv,
    g_send,
    g_recv,
):
    me = lax.axis_index("lat")
    breadth, channels = features_ref.shape[2], features_ref.shape[3]
    cells = 2 * breadth
    tokens = breadth // 2
    chunks = channels // LANES
    group_width = channels // GROUPS
    planes = n // 4

    loads = []
    for a in range(3):
        for b in range(3):
            loads.append((conv1_hbm.at[a, b], w1.at[b, pl.ds(a * channels, channels)]))
    loads.append((affine_hbm, affine))
    split_at = len(loads)
    for a in range(3):
        for b in range(3):
            loads.append((conv2_hbm.at[a, b], w2.at[b, pl.ds(a * channels, channels)]))
    split_too = len(loads)
    loads.append((qkv_hbm, wqkv))
    loads.append((proj_hbm, wproj))
    loads = [pltpu.make_async_copy(s, d, w_sem.at[i]) for i, (s, d) in enumerate(loads)]
    for load in loads:
        load.start()

    barrier = pltpu.get_barrier_semaphore()

    def greet(j, carry):
        pl.semaphore_signal(
            barrier,
            inc=1,
            device_id={"lat": lax.rem(me + j, n)},
            device_id_type=pl.DeviceIdType.MESH,
        )
        return carry

    lax.fori_loop(1, n, greet, 0)

    def remote(src, dst, send, recv, target):
        return pltpu.make_async_remote_copy(
            src_ref=src,
            dst_ref=dst,
            send_sem=send,
            recv_sem=recv,
            device_id={"lat": target},
            device_id_type=pl.DeviceIdType.MESH,
        )

    def tile_of(sums, squares):
        parts = [sums[:, i * LANES : (i + 1) * LANES] for i in range(chunks)]
        parts += [squares[:, i * LANES : (i + 1) * LANES] for i in range(chunks)]
        return jnp.concatenate(parts, axis=0)

    def share_stats(phase):
        def share(j, carry):
            remote(
                stats.at[phase, 0],
                stats.at[phase, j],
                stat_send.at[phase],
                stat_recv.at[phase],
                lax.rem(me + j, n),
            ).start()
            return carry

        lax.fori_loop(1, n, share, 0)

    def wait_stats(phase, sem):
        others = stats.at[phase, pl.ds(1, n - 1)]
        pltpu.make_async_copy(others, others, sem.at[phase]).wait()

    def moments(phase, entries):
        wait_stats(phase, stat_recv)
        sums = group_totals(jnp.sum(stats[phase], axis=0), group_width)
        center = sums[:chunks] / entries
        spread = sums[chunks:] / entries - center * center
        factor = lax.rsqrt(spread + eps)

        def row(t):
            return jnp.concatenate([t[i : i + 1] for i in range(chunks)], axis=1)

        return row(center), row(factor)

    def halo(phase, src, bufs, act):
        @pl.when(me > 0)
        def _():
            act(
                remote(
                    src(0), bufs.at[1], halo_send.at[phase, 0], halo_recv.at[phase, 1], me - 1
                )
            )

        @pl.when(me < n - 1)
        def _():
            act(
                remote(
                    src(1), bufs.at[0], halo_send.at[phase, 1], halo_recv.at[phase, 0], me + 1
                )
            )

    def halo_arrival(phase, bufs, side):
        pltpu.make_async_copy(bufs.at[side], bufs.at[side], halo_recv.at[phase, side]).wait()

    def store_row(k, values):
        for r in range(2):
            if 0 <= k - r < 3:
                abuf[r, :, (k - r) * channels : (k - r + 1) * channels] = values

    def halo_rows(phase, bufs, formula):
        for side, k, inner in ((0, 0, me > 0), (1, 3, me < n - 1)):

            @pl.when(inner)
            def _():
                halo_arrival(phase, bufs, side)
                store_row(k, formula(bufs[side].astype(jnp.float32)))

            @pl.when(jnp.logical_not(inner))
            def _():
                store_row(k, jnp.zeros((breadth, channels), jnp.bfloat16))

    def convolve(weights):
        lhs = abuf[...].reshape(cells, 3 * channels)
        column = lax.rem(lax.broadcasted_iota(jnp.int32, (cells, channels), 0), breadth)
        low = jnp.dot(lhs, weights[0], preferred_element_type=jnp.float32)
        result = jnp.where(column == 0, 0.0, pltpu.roll(low, 1, 0))
        high = jnp.dot(lhs, weights[2], preferred_element_type=jnp.float32)
        result += jnp.where(column == breadth - 1, 0.0, pltpu.roll(high, cells - 1, 0))
        return result + jnp.dot(lhs, weights[1], preferred_element_type=jnp.float32)

    source = features_ref[0].astype(jnp.float32).reshape(cells, channels)
    stats[0, 0] = tile_of(
        jnp.sum(source, axis=0, keepdims=True), jnp.sum(source * source, axis=0, keepdims=True)
    )
    pl.semaphore_wait(barrier, n - 1)
    share_stats(0)

    def feature_row(r):
        return features_ref.at[0, r]

    halo(0, feature_row, halo1, lambda copy: copy.start())

    sigma = jnp.full((8, 2 * FREQS), sigma_ref[noise_ref[0]], jnp.float32)
    lane = lax.broadcasted_iota(jnp.int32, (8, 2 * FREQS), 1)
    order = lax.rem(lane, FREQS).astype(jnp.float32)
    angles = (jnp.log(sigma) / 4.0) * jnp.exp(-math.log(10000.0) * order / FREQS)
    fourier = jnp.where(lane < FREQS, jnp.cos(angles), jnp.sin(angles)).astype(jnp.bfloat16)
    for load in loads[:split_at]:
        load.wait()
    film = jnp.dot(fourier, affine[...], preferred_element_type=jnp.float32)[:1]
    film_scale, film_shift = film[:, :channels], film[:, channels:]

    entries = float(cells * group_width * n)
    center, factor = moments(0, entries)
    scale = factor * gain_ref[0:1]
    offset = bias_ref[0:1]

    def active(values):
        return silu((values - center) * scale + offset).astype(jnp.bfloat16)

    for r in range(2):
        store_row(r + 1, active(features_ref[0, r].astype(jnp.float32)))
    halo_rows(0, halo1, active)

    first_conv = convolve(w1) + conv_bias_ref[0:1]
    first[...] = first_conv
    edges[...] = first_conv.astype(jnp.bfloat16).reshape(2, breadth, channels)
    stats[1, 0] = tile_of(
        jnp.sum(first_conv, axis=0, keepdims=True),
        jnp.sum(first_conv * first_conv, axis=0, keepdims=True),
    )
    share_stats(1)

    def edge_row(r):
        return edges.at[r]

    halo(1, edge_row, halo2, lambda copy: copy.start())
    for load in loads[split_at:split_too]:
        load.wait()
    center1, factor1 = moments(1, entries)
    scale1 = factor1 * gain_ref[1:2]
    offset1 = bias_ref[1:2]

    def middle(values):
        normed = (values - center1) * scale1 + offset1
        return silu(normed * (1.0 + film_scale) + film_shift).astype(jnp.bfloat16)

    for r in range(2):
        store_row(r + 1, middle(first[r * breadth : (r + 1) * breadth]))
    halo_rows(1, halo2, middle)

    second = convolve(w2) + conv_bias_ref[1:2]
    source = features_ref[0].astype(jnp.float32).reshape(cells, channels)
    level_one = ((source + second) * skip_gain).astype(jnp.bfloat16)
    cell = lax.rem(lax.broadcasted_iota(jnp.int32, (tokens, cells), 1), breadth)
    token = lax.broadcasted_iota(jnp.int32, (tokens, cells), 0)
    blocks = jnp.where(cell // 2 == token, 1.0, 0.0).astype(jnp.bfloat16)
    pooled = jnp.dot(blocks, level_one, preferred_element_type=jnp.float32) * 0.25
    pooled_ref[...] = pooled
    stats[2, 0] = tile_of(
        jnp.sum(pooled, axis=0, keepdims=True), jnp.sum(pooled * pooled, axis=0, keepdims=True)
    )
    share_stats(2)

    plane, side, core = me // 4, lax.rem(me // 2, 2), lax.rem(me, 2)
    gath[me] = pooled.astype(jnp.bfloat16)

    def shard(p, s, c):
        return p * 4 + s * 2 + c

    def pass_on(k, way):
        target = (me + 4, me - 4, shard(plane, 1 - side, core), shard(plane, side, 1 - core))[way]
        return remote(gath.at[k], gath.at[k], g_send.at[way, k], g_recv.at[k], target)

    def arrival(k):
        pltpu.make_async_copy(gath.at[k], gath.at[k], g_recv.at[k]).wait()

    def own_band(act):
        @pl.when(plane < planes - 1)
        def _():
            act(pass_on(me, 0))

        @pl.when(plane > 0)
        def _():
            act(pass_on(me, 1))

        act(pass_on(me, 2))
        act(pass_on(me, 3))

    own_band(lambda copy: copy.start())

    def spot(s):
        distance = (s + 1) // 2
        below = lax.rem(s, 2)
        p = plane + distance * (1 - 2 * below)
        valid = (p >= 0) & (p < planes)
        return p, below, valid

    def relay(s, act, waits):
        p, below, valid = spot(s)
        k = shard(p, side, core)

        @pl.when(valid & (s > 0))
        def _():
            if waits:
                arrival(k)

            @pl.when((below == 1) & (plane < planes - 1))
            def _():
                act(pass_on(k, 0))

            @pl.when((below == 0) & (plane > 0))
            def _():
                act(pass_on(k, 1))

            act(pass_on(k, 2))
            act(pass_on(k, 3))

    steps = 2 * planes - 1
    if steps > 1:
        relay(1, lambda copy: copy.start(), True)
        relay(2, lambda copy: copy.start(), True)

    for load in loads[split_too:]:
        load.wait()
    center2, factor2 = moments(2, float(tokens * group_width * n))
    scale2 = factor2 * gain_ref[2:3]
    offset2 = bias_ref[2:3]

    def normed(values):
        return ((values - center2) * scale2 + offset2).astype(jnp.bfloat16)

    wide = 4 * HEAD_DIM
    halves = channels // wide
    head_lane = lax.broadcasted_iota(jnp.int32, (tokens, wide), 1) // HEAD_DIM
    queries = jnp.dot(
        normed(pooled_ref[...]), wqkv[:, :channels], preferred_element_type=jnp.float32
    ).astype(jnp.bfloat16).astype(jnp.float32) * HEAD_DIM ** (-0.5)
    for g in range(halves):
        part = queries[:, g * wide : (g + 1) * wide]
        for i in range(4):
            qm[g, i * tokens : (i + 1) * tokens] = jnp.where(head_lane == i, part, 0.0).astype(
                jnp.bfloat16
            )
    top[...] = jnp.full(top.shape, -1e30, jnp.float32)
    total[...] = jnp.zeros(total.shape, jnp.float32)
    acc[...] = jnp.zeros(acc.shape, jnp.float32)

    def attend(s, carry):
        @pl.when(s + 2 < steps)
        def _():
            @pl.when(s > 0)
            def _():
                relay(s + 2, lambda copy: copy.start(), True)

        p, below, valid = spot(s)

        @pl.when(valid)
        def _():
            across = shard(p, 1 - side, core)
            arrival(across)
            pass_on(across, 3).start()
            arrival(shard(p, side, 1 - core))
            arrival(shard(p, 1 - side, 1 - core))
            rows = gath[pl.ds(p * 4, 4)].astype(jnp.float32).reshape(4 * tokens, channels)
            pairs = jnp.dot(
                normed(rows), wqkv[:, channels:], preferred_element_type=jnp.float32
            ).astype(jnp.bfloat16)
            for g in range(halves):
                keys = pairs[:, g * wide : (g + 1) * wide]
                values = pairs[:, channels + g * wide : channels + (g + 1) * wide]
                scores = lax.dot_general(
                    qm[g], keys, (((1,), (1,)), ((), ())), preferred_element_type=jnp.float32
                )
                old = top[g]
                rising = jnp.maximum(old, jnp.max(scores, axis=1, keepdims=True))
                fading = jnp.exp(old - rising)
                weights = jnp.exp(scores - rising)
                top[g] = rising
                total[g] = total[g] * fading + jnp.sum(weights, axis=1, keepdims=True)
                acc[g] = acc[g] * fading + jnp.dot(
                    weights.astype(jnp.bfloat16), values, preferred_element_type=jnp.float32
                )

        return carry

    lax.fori_loop(0, steps, attend, 0)

    attended = []
    for g in range(halves):
        mixed = acc[g] / total[g]
        part = jnp.zeros((tokens, wide), jnp.float32)
        for i in range(4):
            part = jnp.where(head_lane == i, mixed[i * tokens : (i + 1) * tokens], part)
        attended.append(part.astype(jnp.bfloat16))
    projected = jnp.dot(
        jnp.concatenate(attended, axis=1), wproj[...], preferred_element_type=jnp.float32
    )
    out_ref[0, 0] = ((pooled_ref[...] + projected + proj_bias_ref[...]) * skip_gain).astype(
        jnp.bfloat16
    )

    for phase in range(3):
        wait_stats(phase, stat_send)
    halo(0, feature_row, halo1, lambda copy: copy.wait_send())
    halo(1, edge_row, halo2, lambda copy: copy.wait_send())
    own_band(lambda copy: copy.wait_send())

    def settle(s, carry):
        relay(s, lambda copy: copy.wait_send(), False)
        p, below, valid = spot(s)

        @pl.when(valid)
        def _():
            pass_on(shard(p, 1 - side, core), 3).wait_send()

        return carry

    lax.fori_loop(0, steps, settle, 0)


def solution(mesh):
    n = mesh.shape["lat"]

    def local(
        features,
        noise_index,
        sigma_table,
        affine_weight,
        norm_gain,
        norm_bias,
        conv1_weight,
        conv2_weight,
        conv_bias,
        qkv_weight,
        proj_weight,
        proj_bias,
    ):
        breadth, channels = features.shape[2], features.shape[3]
        tokens = breadth // 2
        wide = 4 * HEAD_DIM
        halves = channels // wide
        bf16, f32 = jnp.bfloat16, jnp.float32
        smem = pl.BlockSpec(memory_space=pltpu.SMEM)
        vmem = pl.BlockSpec(memory_space=pltpu.VMEM)
        hbm = pl.BlockSpec(memory_space=pl.ANY)
        dma = pltpu.SemaphoreType.DMA

        def run(*refs):
            kernel(n, *refs)

        return pl.pallas_call(
            run,
            out_shape=jax.ShapeDtypeStruct((1, 1, tokens, channels), bf16),
            in_specs=[smem, smem, vmem, hbm, vmem, vmem, hbm, hbm, vmem, hbm, hbm, vmem],
            out_specs=vmem,
            scratch_shapes=[
                pltpu.VMEM(affine_weight.shape, bf16),
                pltpu.VMEM((3, 3 * channels, channels), bf16),
                pltpu.VMEM((3, 3 * channels, channels), bf16),
                pltpu.VMEM(qkv_weight.shape, bf16),
                pltpu.VMEM(proj_weight.shape, bf16),
                pltpu.VMEM((2, breadth, 3 * channels), bf16),
                pltpu.VMEM((2 * breadth, channels), f32),
                pltpu.VMEM((2, breadth, channels), bf16),
                pltpu.VMEM((2, breadth, channels), bf16),
                pltpu.VMEM((2, breadth, channels), bf16),
                pltpu.VMEM((3, n, 2 * channels // LANES, LANES), f32),
                pltpu.VMEM((n, tokens, channels), bf16),
                pltpu.VMEM((tokens, channels), f32),
                pltpu.VMEM((halves, 4 * tokens, wide), bf16),
                pltpu.VMEM((halves, 4 * tokens, 1), f32),
                pltpu.VMEM((halves, 4 * tokens, 1), f32),
                pltpu.VMEM((halves, 4 * tokens, wide), f32),
                dma((21,)),
                dma((3,)),
                dma((3,)),
                dma((2, 2)),
                dma((2, 2)),
                dma((4, n)),
                dma((n,)),
            ],
            compiler_params=pltpu.CompilerParams(
                collective_id=0, has_side_effects=True, vmem_limit_bytes=52 * 1024 * 1024
            ),
        )(
            noise_index,
            sigma_table,
            features,
            affine_weight,
            norm_gain,
            norm_bias,
            conv1_weight,
            conv2_weight,
            conv_bias,
            qkv_weight,
            proj_weight,
            proj_bias.reshape(1, channels),
        )

    return jax.shard_map(
        local,
        mesh=mesh,
        in_specs=(P("grp", "lat", None, None), P("grp")) + (P(),) * 10,
        out_specs=P("grp", "lat", None, None),
        check_vma=False,
    )
```

```python
import math

import jax
import jax.numpy as jnp
from jax import lax
from jax.experimental import pallas as pl
from jax.experimental.pallas import tpu as pltpu
from jax.sharding import PartitionSpec as P

HEAD_DIM = 64
GROUPS = 32
FREQS = 64
LANES = 128

eps = 1e-05
skip_gain = 0.7071067811865476


def group_totals(sums, group_width):
    lane = lax.broadcasted_iota(jnp.int32, sums.shape, 1)
    step = 1
    while step < group_width:
        ahead = pltpu.roll(sums, LANES - step, 1)
        behind = pltpu.roll(sums, step, 1)
        sums = sums + jnp.where((lane // step) % 2 == 0, ahead, behind)
        step *= 2
    return sums


def silu(values):
    return values / (1.0 + jnp.exp(-values))


def kernel(
    n,
    noise_hbm,
    sigma_hbm,
    features_hbm,
    affine_hbm,
    gain_hbm,
    bias_hbm,
    conv1_hbm,
    conv2_hbm,
    conv_bias_hbm,
    qkv_hbm,
    proj_hbm,
    proj_bias_hbm,
    out_ref,
    noise_ref,
    sigma_ref,
    features_ref,
    gain_ref,
    bias_ref,
    conv_bias_ref,
    proj_bias_ref,
    affine,
    w1,
    w2,
    wqkv,
    wproj,
    abuf,
    first,
    edges,
    halo1,
    halo2,
    stats,
    gath,
    pooled_ref,
    qm,
    top,
    total,
    acc,
    w_sem,
    stat_send,
    stat_recv,
    halo_send,
    halo_recv,
    g_send,
    g_recv,
):
    me = lax.axis_index("lat")
    breadth, channels = features_ref.shape[2], features_ref.shape[3]
    cells = 2 * breadth
    tokens = breadth // 2
    chunks = channels // LANES
    group_width = channels // GROUPS
    planes = n // 4

    loads = [
        (features_hbm, features_ref),
        (noise_hbm, noise_ref),
        (sigma_hbm, sigma_ref),
        (gain_hbm, gain_ref),
        (bias_hbm, bias_ref),
        (conv_bias_hbm, conv_bias_ref),
        (proj_bias_hbm, proj_bias_ref),
    ]
    for a in range(3):
        for b in range(3):
            loads.append((conv1_hbm.at[a, b], w1.at[b, pl.ds(a * channels, channels)]))
    loads.append((affine_hbm, affine))
    split_at = len(loads)
    for a in range(3):
        for b in range(3):
            loads.append((conv2_hbm.at[a, b], w2.at[b, pl.ds(a * channels, channels)]))
    split_too = len(loads)
    loads.append((qkv_hbm, wqkv))
    loads.append((proj_hbm, wproj))
    loads = [pltpu.make_async_copy(s, d, w_sem.at[i]) for i, (s, d) in enumerate(loads)]
    for load in loads:
        load.start()

    barrier = pltpu.get_barrier_semaphore()

    def greet(j, carry):
        pl.semaphore_signal(
            barrier,
            inc=1,
            device_id={"lat": lax.rem(me + j, n)},
            device_id_type=pl.DeviceIdType.MESH,
        )
        return carry

    lax.fori_loop(1, n, greet, 0)

    def remote(src, dst, send, recv, target):
        return pltpu.make_async_remote_copy(
            src_ref=src,
            dst_ref=dst,
            send_sem=send,
            recv_sem=recv,
            device_id={"lat": target},
            device_id_type=pl.DeviceIdType.MESH,
        )

    def tile_of(sums, squares):
        parts = [sums[:, i * LANES : (i + 1) * LANES] for i in range(chunks)]
        parts += [squares[:, i * LANES : (i + 1) * LANES] for i in range(chunks)]
        return jnp.concatenate(parts, axis=0)

    def share_stats(phase):
        def share(j, carry):
            remote(
                stats.at[phase, 0],
                stats.at[phase, j],
                stat_send.at[phase],
                stat_recv.at[phase],
                lax.rem(me + j, n),
            ).start()
            return carry

        lax.fori_loop(1, n, share, 0)

    def wait_stats(phase, sem):
        others = stats.at[phase, pl.ds(1, n - 1)]
        pltpu.make_async_copy(others, others, sem.at[phase]).wait()

    def moments(phase, entries):
        wait_stats(phase, stat_recv)
        sums = group_totals(jnp.sum(stats[phase], axis=0), group_width)
        center = sums[:chunks] / entries
        spread = sums[chunks:] / entries - center * center
        factor = lax.rsqrt(spread + eps)

        def row(t):
            return jnp.concatenate([t[i : i + 1] for i in range(chunks)], axis=1)

        return row(center), row(factor)

    def halo(phase, src, bufs, act):
        @pl.when(me > 0)
        def _():
            act(
                remote(
                    src(0), bufs.at[1], halo_send.at[phase, 0], halo_recv.at[phase, 1], me - 1
                )
            )

        @pl.when(me < n - 1)
        def _():
            act(
                remote(
                    src(1), bufs.at[0], halo_send.at[phase, 1], halo_recv.at[phase, 0], me + 1
                )
            )

    def halo_arrival(phase, bufs, side):
        pltpu.make_async_copy(bufs.at[side], bufs.at[side], halo_recv.at[phase, side]).wait()

    def store_row(k, values):
        for r in range(2):
            if 0 <= k - r < 3:
                abuf[r, :, (k - r) * channels : (k - r + 1) * channels] = values

    def halo_rows(phase, bufs, formula):
        for side, k, inner in ((0, 0, me > 0), (1, 3, me < n - 1)):

            @pl.when(inner)
            def _():
                halo_arrival(phase, bufs, side)
                store_row(k, formula(bufs[side].astype(jnp.float32)))

            @pl.when(jnp.logical_not(inner))
            def _():
                store_row(k, jnp.zeros((breadth, channels), jnp.bfloat16))

    def taps(lhs, weights, a, depth):
        rows = lhs.shape[0]
        column = lax.rem(lax.broadcasted_iota(jnp.int32, (rows, channels), 0), breadth)
        part = [
            jnp.dot(
                lhs,
                weights[b, a * channels : (a + depth) * channels],
                preferred_element_type=jnp.float32,
            )
            for b in range(3)
        ]
        low = jnp.where(column == 0, 0.0, pltpu.roll(part[0], 1, 0))
        high = jnp.where(column == breadth - 1, 0.0, pltpu.roll(part[2], rows - 1, 0))
        return low + high + part[1]

    def convolve_own(weights):
        for r in range(2):
            lhs = abuf[r, :, (1 - r) * channels : (3 - r) * channels]
            first[r * breadth : (r + 1) * breadth] = taps(lhs, weights, 1 - r, 2)

    def convolve_rest(weights, r):
        lhs = abuf[r, :, 2 * r * channels : (2 * r + 1) * channels]
        return first[r * breadth : (r + 1) * breadth] + taps(lhs, weights, 2 * r, 1)

    loads[0].wait()
    source = features_ref[0].astype(jnp.float32).reshape(cells, channels)
    stats[0, 0] = tile_of(
        jnp.sum(source, axis=0, keepdims=True), jnp.sum(source * source, axis=0, keepdims=True)
    )
    pl.semaphore_wait(barrier, n - 1)
    share_stats(0)

    def feature_row(r):
        return features_ref.at[0, r]

    halo(0, feature_row, halo1, lambda copy: copy.start())

    for load in loads[1:split_at]:
        load.wait()
    sigma = jnp.full((8, 2 * FREQS), sigma_ref[noise_ref[0]], jnp.float32)
    lane = lax.broadcasted_iota(jnp.int32, (8, 2 * FREQS), 1)
    order = lax.rem(lane, FREQS).astype(jnp.float32)
    angles = (jnp.log(sigma) / 4.0) * jnp.exp(-math.log(10000.0) * order / FREQS)
    fourier = jnp.where(lane < FREQS, jnp.cos(angles), jnp.sin(angles)).astype(jnp.bfloat16)
    film = jnp.dot(fourier, affine[...], preferred_element_type=jnp.float32)[:1]
    film_scale, film_shift = film[:, :channels], film[:, channels:]

    entries = float(cells * group_width * n)
    center, factor = moments(0, entries)
    scale = factor * gain_ref[0:1]
    offset = bias_ref[0:1]

    def active(values):
        return silu((values - center) * scale + offset).astype(jnp.bfloat16)

    for r in range(2):
        store_row(r + 1, active(features_ref[0, r].astype(jnp.float32)))
    convolve_own(w1)
    halo_rows(0, halo1, active)

    first_conv = (
        jnp.concatenate([convolve_rest(w1, r) for r in range(2)], axis=0) + conv_bias_ref[0:1]
    )
    first[...] = first_conv
    edges[...] = first_conv.astype(jnp.bfloat16).reshape(2, breadth, channels)
    stats[1, 0] = tile_of(
        jnp.sum(first_conv, axis=0, keepdims=True),
        jnp.sum(first_conv * first_conv, axis=0, keepdims=True),
    )
    share_stats(1)

    def edge_row(r):
        return edges.at[r]

    halo(1, edge_row, halo2, lambda copy: copy.start())
    for load in loads[split_at:split_too]:
        load.wait()
    center1, factor1 = moments(1, entries)
    scale1 = factor1 * gain_ref[1:2]
    offset1 = bias_ref[1:2]

    def middle(values):
        normed = (values - center1) * scale1 + offset1
        return silu(normed * (1.0 + film_scale) + film_shift).astype(jnp.bfloat16)

    for r in range(2):
        store_row(r + 1, middle(first[r * breadth : (r + 1) * breadth]))
    convolve_own(w2)
    halo_rows(1, halo2, middle)

    second = (
        jnp.concatenate([convolve_rest(w2, r) for r in range(2)], axis=0) + conv_bias_ref[1:2]
    )
    source = features_ref[0].astype(jnp.float32).reshape(cells, channels)
    level_one = ((source + second) * skip_gain).astype(jnp.bfloat16)
    cell = lax.rem(lax.broadcasted_iota(jnp.int32, (tokens, cells), 1), breadth)
    token = lax.broadcasted_iota(jnp.int32, (tokens, cells), 0)
    blocks = jnp.where(cell // 2 == token, 1.0, 0.0).astype(jnp.bfloat16)
    pooled = jnp.dot(blocks, level_one, preferred_element_type=jnp.float32) * 0.25
    pooled_ref[...] = pooled
    stats[2, 0] = tile_of(
        jnp.sum(pooled, axis=0, keepdims=True), jnp.sum(pooled * pooled, axis=0, keepdims=True)
    )
    share_stats(2)

    plane, side, core = me // 4, lax.rem(me // 2, 2), lax.rem(me, 2)
    gath[me] = pooled.astype(jnp.bfloat16)

    def shard(p, s, c):
        return p * 4 + s * 2 + c

    pieces = 2 if tokens % 32 == 0 else 1
    piece = tokens // pieces

    def pass_on(k, way, h):
        target = (me + 4, me - 4, shard(plane, 1 - side, core), shard(plane, side, 1 - core))[way]
        band = gath.at[k, pl.ds(h * piece, piece)]
        return remote(band, band, g_send.at[way, k, h], g_recv.at[k, h], target)

    def arrival(k, h):
        band = gath.at[k, pl.ds(h * piece, piece)]
        pltpu.make_async_copy(band, band, g_recv.at[k, h]).wait()

    def own_band(act):
        for h in range(pieces):

            @pl.when(plane < planes - 1)
            def _():
                act(pass_on(me, 0, h))

            @pl.when(plane > 0)
            def _():
                act(pass_on(me, 1, h))

            act(pass_on(me, 2, h))
            act(pass_on(me, 3, h))

    own_band(lambda copy: copy.start())

    def spot(s):
        distance = (s + 1) // 2
        below = lax.rem(s, 2)
        p = plane + distance * (1 - 2 * below)
        valid = (p >= 0) & (p < planes)
        return p, below, valid

    def relay(s, act, waits):
        p, below, valid = spot(s)
        k = shard(p, side, core)

        @pl.when(valid & (s > 0))
        def _():
            for h in range(pieces):
                if waits:
                    arrival(k, h)

                @pl.when((below == 1) & (plane < planes - 1))
                def _():
                    act(pass_on(k, 0, h))

                @pl.when((below == 0) & (plane > 0))
                def _():
                    act(pass_on(k, 1, h))

                act(pass_on(k, 2, h))
                act(pass_on(k, 3, h))

    steps = 2 * planes - 1
    if steps > 1:
        relay(1, lambda copy: copy.start(), True)
        relay(2, lambda copy: copy.start(), True)

    for load in loads[split_too:]:
        load.wait()
    center2, factor2 = moments(2, float(tokens * group_width * n))
    scale2 = factor2 * gain_ref[2:3]
    offset2 = bias_ref[2:3]

    def normed(values):
        return ((values - center2) * scale2 + offset2).astype(jnp.bfloat16)

    wide = 4 * HEAD_DIM
    halves = channels // wide
    head_lane = lax.broadcasted_iota(jnp.int32, (tokens, wide), 1) // HEAD_DIM
    queries = jnp.dot(
        normed(pooled_ref[...]), wqkv[:, :channels], preferred_element_type=jnp.float32
    ).astype(jnp.bfloat16).astype(jnp.float32) * HEAD_DIM ** (-0.5)
    for g in range(halves):
        part = queries[:, g * wide : (g + 1) * wide]
        for i in range(4):
            qm[g, i * tokens : (i + 1) * tokens] = jnp.where(head_lane == i, part, 0.0).astype(
                jnp.bfloat16
            )
    top[...] = jnp.full(top.shape, -1e30, jnp.float32)
    total[...] = jnp.zeros(total.shape, jnp.float32)
    acc[...] = jnp.zeros(acc.shape, jnp.float32)

    def attend(s, carry):
        @pl.when(s + 2 < steps)
        def _():
            @pl.when(s > 0)
            def _():
                relay(s + 2, lambda copy: copy.start(), True)

        p, below, valid = spot(s)

        @pl.when(valid)
        def _():
            across = shard(p, 1 - side, core)
            for h in range(pieces):
                arrival(across, h)
                pass_on(across, 3, h).start()
            for h in range(pieces):
                arrival(shard(p, side, 1 - core), h)
                arrival(shard(p, 1 - side, 1 - core), h)
            rows = gath[pl.ds(p * 4, 4)].astype(jnp.float32).reshape(4 * tokens, channels)
            pairs = jnp.dot(
                normed(rows), wqkv[:, channels:], preferred_element_type=jnp.float32
            ).astype(jnp.bfloat16)
            for g in range(halves):
                keys = pairs[:, g * wide : (g + 1) * wide]
                values = pairs[:, channels + g * wide : channels + (g + 1) * wide]
                scores = lax.dot_general(
                    qm[g], keys, (((1,), (1,)), ((), ())), preferred_element_type=jnp.float32
                )
                old = top[g]
                rising = jnp.maximum(old, jnp.max(scores, axis=1, keepdims=True))
                fading = jnp.exp(old - rising)
                weights = jnp.exp(scores - rising)
                top[g] = rising
                total[g] = total[g] * fading + jnp.sum(weights, axis=1, keepdims=True)
                acc[g] = acc[g] * fading + jnp.dot(
                    weights.astype(jnp.bfloat16), values, preferred_element_type=jnp.float32
                )

        return carry

    lax.fori_loop(0, steps, attend, 0)

    attended = []
    for g in range(halves):
        mixed = acc[g] / total[g]
        part = jnp.zeros((tokens, wide), jnp.float32)
        for i in range(4):
            part = jnp.where(head_lane == i, mixed[i * tokens : (i + 1) * tokens], part)
        attended.append(part.astype(jnp.bfloat16))
    projected = jnp.dot(
        jnp.concatenate(attended, axis=1), wproj[...], preferred_element_type=jnp.float32
    )
    out_ref[0, 0] = ((pooled_ref[...] + projected + proj_bias_ref[...]) * skip_gain).astype(
        jnp.bfloat16
    )

    for phase in range(3):
        wait_stats(phase, stat_send)
    halo(0, feature_row, halo1, lambda copy: copy.wait_send())
    halo(1, edge_row, halo2, lambda copy: copy.wait_send())
    own_band(lambda copy: copy.wait_send())

    def settle(s, carry):
        relay(s, lambda copy: copy.wait_send(), False)
        p, below, valid = spot(s)

        @pl.when(valid)
        def _():
            for h in range(pieces):
                pass_on(shard(p, 1 - side, core), 3, h).wait_send()

        return carry

    lax.fori_loop(0, steps, settle, 0)


def solution(mesh):
    n = mesh.shape["lat"]

    def local(
        features,
        noise_index,
        sigma_table,
        affine_weight,
        norm_gain,
        norm_bias,
        conv1_weight,
        conv2_weight,
        conv_bias,
        qkv_weight,
        proj_weight,
        proj_bias,
    ):
        breadth, channels = features.shape[2], features.shape[3]
        tokens = breadth // 2
        wide = 4 * HEAD_DIM
        halves = channels // wide
        bf16, f32 = jnp.bfloat16, jnp.float32
        vmem = pl.BlockSpec(memory_space=pltpu.VMEM)
        hbm = pl.BlockSpec(memory_space=pltpu.HBM)
        dma = pltpu.SemaphoreType.DMA

        def run(*refs):
            kernel(n, *refs)

        return pl.pallas_call(
            run,
            out_shape=jax.ShapeDtypeStruct((1, 1, tokens, channels), bf16),
            in_specs=[hbm] * 12,
            out_specs=vmem,
            scratch_shapes=[
                pltpu.SMEM(noise_index.shape, jnp.int32),
                pltpu.SMEM(sigma_table.shape, f32),
                pltpu.VMEM(features.shape, bf16),
                pltpu.VMEM(norm_gain.shape, f32),
                pltpu.VMEM(norm_bias.shape, f32),
                pltpu.VMEM(conv_bias.shape, f32),
                pltpu.VMEM((1, channels), f32),
                pltpu.VMEM(affine_weight.shape, bf16),
                pltpu.VMEM((3, 3 * channels, channels), bf16),
                pltpu.VMEM((3, 3 * channels, channels), bf16),
                pltpu.VMEM(qkv_weight.shape, bf16),
                pltpu.VMEM(proj_weight.shape, bf16),
                pltpu.VMEM((2, breadth, 3 * channels), bf16),
                pltpu.VMEM((2 * breadth, channels), f32),
                pltpu.VMEM((2, breadth, channels), bf16),
                pltpu.VMEM((2, breadth, channels), bf16),
                pltpu.VMEM((2, breadth, channels), bf16),
                pltpu.VMEM((3, n, 2 * channels // LANES, LANES), f32),
                pltpu.VMEM((n, tokens, channels), bf16),
                pltpu.VMEM((tokens, channels), f32),
                pltpu.VMEM((halves, 4 * tokens, wide), bf16),
                pltpu.VMEM((halves, 4 * tokens, 1), f32),
                pltpu.VMEM((halves, 4 * tokens, 1), f32),
                pltpu.VMEM((halves, 4 * tokens, wide), f32),
                dma((28,)),
                dma((3,)),
                dma((3,)),
                dma((2, 2)),
                dma((2, 2)),
                dma((4, n, 2)),
                dma((n, 2)),
            ],
            compiler_params=pltpu.CompilerParams(
                collective_id=0, has_side_effects=True, vmem_limit_bytes=64 * 1024 * 1024
            ),
        )(
            noise_index,
            sigma_table,
            features,
            affine_weight,
            norm_gain,
            norm_bias,
            conv1_weight,
            conv2_weight,
            conv_bias,
            qkv_weight,
            proj_weight,
            proj_bias.reshape(1, channels),
        )

    return jax.shard_map(
        local,
        mesh=mesh,
        in_specs=(P("grp", "lat", None, None), P("grp")) + (P(),) * 10,
        out_specs=P("grp", "lat", None, None),
        check_vma=False,
    )
```

```python
import math

import jax
import jax.numpy as jnp
from jax import lax
from jax.experimental import pallas as pl
from jax.experimental.pallas import tpu as pltpu
from jax.sharding import PartitionSpec as P

HEAD_DIM = 64
GROUPS = 32
FREQS = 64
LANES = 128

eps = 1e-05
skip_gain = 0.7071067811865476


def group_totals(sums, group_width):
    lane = lax.broadcasted_iota(jnp.int32, sums.shape, 1)
    step = 1
    while step < group_width:
        ahead = pltpu.roll(sums, LANES - step, 1)
        behind = pltpu.roll(sums, step, 1)
        sums = sums + jnp.where((lane // step) % 2 == 0, ahead, behind)
        step *= 2
    return sums


def silu(values):
    return values / (1.0 + jnp.exp(-values))


def kernel(
    n,
    noise_hbm,
    sigma_hbm,
    features_hbm,
    affine_hbm,
    gain_hbm,
    bias_hbm,
    conv1_hbm,
    conv2_hbm,
    conv_bias_hbm,
    qkv_hbm,
    proj_hbm,
    proj_bias_hbm,
    out_ref,
    noise_ref,
    sigma_ref,
    features_ref,
    gain_ref,
    bias_ref,
    conv_bias_ref,
    proj_bias_ref,
    affine,
    w1,
    w2,
    wqkv,
    wproj,
    abuf,
    first,
    edges,
    halo1,
    halo2,
    stats,
    gath,
    pooled_ref,
    qm,
    top,
    total,
    acc,
    w_sem,
    stat_send,
    stat_recv,
    halo_send,
    halo_recv,
    g_send,
    g_recv,
):
    me = lax.axis_index("lat")
    breadth, channels = features_ref.shape[2], features_ref.shape[3]
    cells = 2 * breadth
    tokens = breadth // 2
    chunks = channels // LANES
    group_width = channels // GROUPS
    planes = n // 4

    loads = [
        (features_hbm, features_ref),
        (noise_hbm, noise_ref),
        (sigma_hbm, sigma_ref),
        (gain_hbm, gain_ref),
        (bias_hbm, bias_ref),
        (conv_bias_hbm, conv_bias_ref),
        (proj_bias_hbm, proj_bias_ref),
    ]
    for a in range(3):
        for b in range(3):
            loads.append((conv1_hbm.at[a, b], w1.at[b, pl.ds(a * channels, channels)]))
    loads.append((affine_hbm, affine))
    split_at = len(loads)
    for a in range(3):
        for b in range(3):
            loads.append((conv2_hbm.at[a, b], w2.at[b, pl.ds(a * channels, channels)]))
    split_too = len(loads)
    loads.append((qkv_hbm, wqkv))
    loads.append((proj_hbm, wproj))
    loads = [pltpu.make_async_copy(s, d, w_sem.at[i]) for i, (s, d) in enumerate(loads)]
    for load in loads:
        load.start()

    barrier = pltpu.get_barrier_semaphore()

    def greet(j, carry):
        pl.semaphore_signal(
            barrier,
            inc=1,
            device_id={"lat": lax.rem(me + j, n)},
            device_id_type=pl.DeviceIdType.MESH,
        )
        return carry

    lax.fori_loop(1, n, greet, 0, unroll=n <= 16)

    def remote(src, dst, send, recv, target):
        return pltpu.make_async_remote_copy(
            src_ref=src,
            dst_ref=dst,
            send_sem=send,
            recv_sem=recv,
            device_id={"lat": target},
            device_id_type=pl.DeviceIdType.MESH,
        )

    def tile_of(sums, squares):
        parts = [sums[:, i * LANES : (i + 1) * LANES] for i in range(chunks)]
        parts += [squares[:, i * LANES : (i + 1) * LANES] for i in range(chunks)]
        return jnp.concatenate(parts, axis=0)

    def share_stats(phase):
        def share(j, carry):
            remote(
                stats.at[phase, 0],
                stats.at[phase, j],
                stat_send.at[phase],
                stat_recv.at[phase],
                lax.rem(me + j, n),
            ).start()
            return carry

        lax.fori_loop(1, n, share, 0, unroll=n <= 16)

    def wait_stats(phase, sem):
        others = stats.at[phase, pl.ds(1, n - 1)]
        pltpu.make_async_copy(others, others, sem.at[phase]).wait()

    def moments(phase, entries):
        wait_stats(phase, stat_recv)
        sums = group_totals(jnp.sum(stats[phase], axis=0), group_width)
        center = sums[:chunks] / entries
        spread = sums[chunks:] / entries - center * center
        factor = lax.rsqrt(spread + eps)

        def row(t):
            return jnp.concatenate([t[i : i + 1] for i in range(chunks)], axis=1)

        return row(center), row(factor)

    def halo(phase, src, bufs, act):
        @pl.when(me > 0)
        def _():
            act(
                remote(
                    src(0), bufs.at[1], halo_send.at[phase, 0], halo_recv.at[phase, 1], me - 1
                )
            )

        @pl.when(me < n - 1)
        def _():
            act(
                remote(
                    src(1), bufs.at[0], halo_send.at[phase, 1], halo_recv.at[phase, 0], me + 1
                )
            )

    def halo_arrival(phase, bufs, side):
        pltpu.make_async_copy(bufs.at[side], bufs.at[side], halo_recv.at[phase, side]).wait()

    def store_row(k, values):
        for r in range(2):
            if 0 <= k - r < 3:
                abuf[r, :, (k - r) * channels : (k - r + 1) * channels] = values

    def halo_rows(phase, bufs, formula):
        for side, k, inner in ((0, 0, me > 0), (1, 3, me < n - 1)):

            @pl.when(inner)
            def _():
                halo_arrival(phase, bufs, side)
                store_row(k, formula(bufs[side].astype(jnp.float32)))

            @pl.when(jnp.logical_not(inner))
            def _():
                store_row(k, jnp.zeros((breadth, channels), jnp.bfloat16))

    def taps(lhs, weights, a, depth):
        rows = lhs.shape[0]
        column = lax.rem(lax.broadcasted_iota(jnp.int32, (rows, channels), 0), breadth)
        part = [
            jnp.dot(
                lhs,
                weights[b, a * channels : (a + depth) * channels],
                preferred_element_type=jnp.float32,
            )
            for b in range(3)
        ]
        low = jnp.where(column == 0, 0.0, pltpu.roll(part[0], 1, 0))
        high = jnp.where(column == breadth - 1, 0.0, pltpu.roll(part[2], rows - 1, 0))
        return low + high + part[1]

    def convolve_own(weights):
        for r in range(2):
            lhs = abuf[r, :, (1 - r) * channels : (3 - r) * channels]
            first[r * breadth : (r + 1) * breadth] = taps(lhs, weights, 1 - r, 2)

    def convolve_rest(weights, r):
        lhs = abuf[r, :, 2 * r * channels : (2 * r + 1) * channels]
        return first[r * breadth : (r + 1) * breadth] + taps(lhs, weights, 2 * r, 1)

    loads[0].wait()
    source = features_ref[0].astype(jnp.float32).reshape(cells, channels)
    stats[0, 0] = tile_of(
        jnp.sum(source, axis=0, keepdims=True), jnp.sum(source * source, axis=0, keepdims=True)
    )
    pl.semaphore_wait(barrier, n - 1)
    share_stats(0)

    def feature_row(r):
        return features_ref.at[0, r]

    halo(0, feature_row, halo1, lambda copy: copy.start())

    for load in loads[1:split_at]:
        load.wait()
    sigma = jnp.full((8, 2 * FREQS), sigma_ref[noise_ref[0]], jnp.float32)
    lane = lax.broadcasted_iota(jnp.int32, (8, 2 * FREQS), 1)
    order = lax.rem(lane, FREQS).astype(jnp.float32)
    angles = (jnp.log(sigma) / 4.0) * jnp.exp(-math.log(10000.0) * order / FREQS)
    fourier = jnp.where(lane < FREQS, jnp.cos(angles), jnp.sin(angles)).astype(jnp.bfloat16)
    film = jnp.dot(fourier, affine[...], preferred_element_type=jnp.float32)[:1]
    film_scale, film_shift = film[:, :channels], film[:, channels:]

    entries = float(cells * group_width * n)
    center, factor = moments(0, entries)
    scale = factor * gain_ref[0:1]
    offset = bias_ref[0:1]

    def active(values):
        return silu((values - center) * scale + offset).astype(jnp.bfloat16)

    for r in range(2):
        store_row(r + 1, active(features_ref[0, r].astype(jnp.float32)))
    convolve_own(w1)
    halo_rows(0, halo1, active)

    first_conv = (
        jnp.concatenate([convolve_rest(w1, r) for r in range(2)], axis=0) + conv_bias_ref[0:1]
    )
    first[...] = first_conv
    edges[...] = first_conv.astype(jnp.bfloat16).reshape(2, breadth, channels)
    stats[1, 0] = tile_of(
        jnp.sum(first_conv, axis=0, keepdims=True),
        jnp.sum(first_conv * first_conv, axis=0, keepdims=True),
    )
    share_stats(1)

    def edge_row(r):
        return edges.at[r]

    halo(1, edge_row, halo2, lambda copy: copy.start())
    for load in loads[split_at:split_too]:
        load.wait()
    center1, factor1 = moments(1, entries)
    scale1 = factor1 * gain_ref[1:2]
    offset1 = bias_ref[1:2]

    def middle(values):
        normed = (values - center1) * scale1 + offset1
        return silu(normed * (1.0 + film_scale) + film_shift).astype(jnp.bfloat16)

    for r in range(2):
        store_row(r + 1, middle(first[r * breadth : (r + 1) * breadth]))
    convolve_own(w2)
    halo_rows(1, halo2, middle)

    second = (
        jnp.concatenate([convolve_rest(w2, r) for r in range(2)], axis=0) + conv_bias_ref[1:2]
    )
    source = features_ref[0].astype(jnp.float32).reshape(cells, channels)
    level_one = ((source + second) * skip_gain).astype(jnp.bfloat16)
    cell = lax.rem(lax.broadcasted_iota(jnp.int32, (tokens, cells), 1), breadth)
    token = lax.broadcasted_iota(jnp.int32, (tokens, cells), 0)
    blocks = jnp.where(cell // 2 == token, 1.0, 0.0).astype(jnp.bfloat16)
    pooled = jnp.dot(blocks, level_one, preferred_element_type=jnp.float32) * 0.25
    pooled_ref[...] = pooled
    stats[2, 0] = tile_of(
        jnp.sum(pooled, axis=0, keepdims=True), jnp.sum(pooled * pooled, axis=0, keepdims=True)
    )
    share_stats(2)

    plane, side, core = me // 4, lax.rem(me // 2, 2), lax.rem(me, 2)
    gath[me] = pooled.astype(jnp.bfloat16)

    def shard(p, s, c):
        return p * 4 + s * 2 + c

    pieces = 2 if tokens % 32 == 0 else 1
    piece = tokens // pieces

    def pass_on(k, way, h):
        target = (me + 4, me - 4, shard(plane, 1 - side, core), shard(plane, side, 1 - core))[way]
        band = gath.at[k, pl.ds(h * piece, piece)]
        return remote(band, band, g_send.at[way, k, h], g_recv.at[k, h], target)

    def arrival(k, h):
        band = gath.at[k, pl.ds(h * piece, piece)]
        pltpu.make_async_copy(band, band, g_recv.at[k, h]).wait()

    def own_band(act):
        for h in range(pieces):

            @pl.when(plane < planes - 1)
            def _():
                act(pass_on(me, 0, h))

            @pl.when(plane > 0)
            def _():
                act(pass_on(me, 1, h))

            act(pass_on(me, 2, h))
            act(pass_on(me, 3, h))

    own_band(lambda copy: copy.start())

    def spot(s):
        distance = (s + 1) // 2
        below = lax.rem(s, 2)
        p = plane + distance * (1 - 2 * below)
        valid = (p >= 0) & (p < planes)
        return p, below, valid

    def relay(s, act, waits):
        p, below, valid = spot(s)
        k = shard(p, side, core)

        @pl.when(valid & (s > 0))
        def _():
            for h in range(pieces):
                if waits:
                    arrival(k, h)

                @pl.when((below == 1) & (plane < planes - 1))
                def _():
                    act(pass_on(k, 0, h))

                @pl.when((below == 0) & (plane > 0))
                def _():
                    act(pass_on(k, 1, h))

                act(pass_on(k, 2, h))
                act(pass_on(k, 3, h))

    steps = 2 * planes - 1
    if steps > 1:
        relay(1, lambda copy: copy.start(), True)
        relay(2, lambda copy: copy.start(), True)

    for load in loads[split_too:]:
        load.wait()
    center2, factor2 = moments(2, float(tokens * group_width * n))
    scale2 = factor2 * gain_ref[2:3]
    offset2 = bias_ref[2:3]

    def normed(values):
        return ((values - center2) * scale2 + offset2).astype(jnp.bfloat16)

    wide = 4 * HEAD_DIM
    halves = channels // wide
    head_lane = lax.broadcasted_iota(jnp.int32, (tokens, wide), 1) // HEAD_DIM
    queries = jnp.dot(
        normed(pooled_ref[...]), wqkv[:, :channels], preferred_element_type=jnp.float32
    ).astype(jnp.bfloat16).astype(jnp.float32) * HEAD_DIM ** (-0.5)
    for g in range(halves):
        part = queries[:, g * wide : (g + 1) * wide]
        for i in range(4):
            qm[g, i * tokens : (i + 1) * tokens] = jnp.where(head_lane == i, part, 0.0).astype(
                jnp.bfloat16
            )
    top[...] = jnp.full(top.shape, -1e30, jnp.float32)
    total[...] = jnp.zeros(total.shape, jnp.float32)
    acc[...] = jnp.zeros(acc.shape, jnp.float32)

    if steps > 3:
        relay(3, lambda copy: copy.start(), True)
        relay(4, lambda copy: copy.start(), True)

    def attend(s, carry):
        @pl.when(s + 4 < steps)
        def _():
            @pl.when(s > 0)
            def _():
                relay(s + 4, lambda copy: copy.start(), True)

        p, below, valid = spot(s)

        @pl.when(valid)
        def _():
            across = shard(p, 1 - side, core)
            for h in range(pieces):
                arrival(across, h)
                pass_on(across, 3, h).start()
            for h in range(pieces):
                arrival(shard(p, side, 1 - core), h)
                arrival(shard(p, 1 - side, 1 - core), h)
            rows = gath[pl.ds(p * 4, 4)].astype(jnp.float32).reshape(4 * tokens, channels)
            pairs = jnp.dot(
                normed(rows), wqkv[:, channels:], preferred_element_type=jnp.float32
            ).astype(jnp.bfloat16)
            for g in range(halves):
                keys = pairs[:, g * wide : (g + 1) * wide]
                values = pairs[:, channels + g * wide : channels + (g + 1) * wide]
                scores = lax.dot_general(
                    qm[g], keys, (((1,), (1,)), ((), ())), preferred_element_type=jnp.float32
                )
                old = top[g]
                rising = jnp.maximum(old, jnp.max(scores, axis=1, keepdims=True))
                fading = jnp.exp(old - rising)
                weights = jnp.exp(scores - rising)
                top[g] = rising
                total[g] = total[g] * fading + jnp.sum(weights, axis=1, keepdims=True)
                acc[g] = acc[g] * fading + jnp.dot(
                    weights.astype(jnp.bfloat16), values, preferred_element_type=jnp.float32
                )

        return carry

    lax.fori_loop(0, steps, attend, 0)

    attended = []
    for g in range(halves):
        mixed = acc[g] / total[g]
        part = jnp.zeros((tokens, wide), jnp.float32)
        for i in range(4):
            part = jnp.where(head_lane == i, mixed[i * tokens : (i + 1) * tokens], part)
        attended.append(part.astype(jnp.bfloat16))
    projected = jnp.dot(
        jnp.concatenate(attended, axis=1), wproj[...], preferred_element_type=jnp.float32
    )
    out_ref[0, 0] = ((pooled_ref[...] + projected + proj_bias_ref[...]) * skip_gain).astype(
        jnp.bfloat16
    )

    for phase in range(3):
        wait_stats(phase, stat_send)
    halo(0, feature_row, halo1, lambda copy: copy.wait_send())
    halo(1, edge_row, halo2, lambda copy: copy.wait_send())
    own_band(lambda copy: copy.wait_send())

    def settle(s, carry):
        relay(s, lambda copy: copy.wait_send(), False)
        p, below, valid = spot(s)

        @pl.when(valid)
        def _():
            for h in range(pieces):
                pass_on(shard(p, 1 - side, core), 3, h).wait_send()

        return carry

    lax.fori_loop(0, steps, settle, 0)


def solution(mesh):
    n = mesh.shape["lat"]

    def local(
        features,
        noise_index,
        sigma_table,
        affine_weight,
        norm_gain,
        norm_bias,
        conv1_weight,
        conv2_weight,
        conv_bias,
        qkv_weight,
        proj_weight,
        proj_bias,
    ):
        breadth, channels = features.shape[2], features.shape[3]
        tokens = breadth // 2
        wide = 4 * HEAD_DIM
        halves = channels // wide
        bf16, f32 = jnp.bfloat16, jnp.float32
        vmem = pl.BlockSpec(memory_space=pltpu.VMEM)
        hbm = pl.BlockSpec(memory_space=pltpu.HBM)
        dma = pltpu.SemaphoreType.DMA

        def run(*refs):
            kernel(n, *refs)

        return pl.pallas_call(
            run,
            out_shape=jax.ShapeDtypeStruct((1, 1, tokens, channels), bf16),
            in_specs=[hbm] * 12,
            out_specs=vmem,
            scratch_shapes=[
                pltpu.SMEM(noise_index.shape, jnp.int32),
                pltpu.SMEM(sigma_table.shape, f32),
                pltpu.VMEM(features.shape, bf16),
                pltpu.VMEM(norm_gain.shape, f32),
                pltpu.VMEM(norm_bias.shape, f32),
                pltpu.VMEM(conv_bias.shape, f32),
                pltpu.VMEM((1, channels), f32),
                pltpu.VMEM(affine_weight.shape, bf16),
                pltpu.VMEM((3, 3 * channels, channels), bf16),
                pltpu.VMEM((3, 3 * channels, channels), bf16),
                pltpu.VMEM(qkv_weight.shape, bf16),
                pltpu.VMEM(proj_weight.shape, bf16),
                pltpu.VMEM((2, breadth, 3 * channels), bf16),
                pltpu.VMEM((2 * breadth, channels), f32),
                pltpu.VMEM((2, breadth, channels), bf16),
                pltpu.VMEM((2, breadth, channels), bf16),
                pltpu.VMEM((2, breadth, channels), bf16),
                pltpu.VMEM((3, n, 2 * channels // LANES, LANES), f32),
                pltpu.VMEM((n, tokens, channels), bf16),
                pltpu.VMEM((tokens, channels), f32),
                pltpu.VMEM((halves, 4 * tokens, wide), bf16),
                pltpu.VMEM((halves, 4 * tokens, 1), f32),
                pltpu.VMEM((halves, 4 * tokens, 1), f32),
                pltpu.VMEM((halves, 4 * tokens, wide), f32),
                dma((28,)),
                dma((3,)),
                dma((3,)),
                dma((2, 2)),
                dma((2, 2)),
                dma((4, n, 2)),
                dma((n, 2)),
            ],
            compiler_params=pltpu.CompilerParams(
                collective_id=0, has_side_effects=True, vmem_limit_bytes=64 * 1024 * 1024
            ),
        )(
            noise_index,
            sigma_table,
            features,
            affine_weight,
            norm_gain,
            norm_bias,
            conv1_weight,
            conv2_weight,
            conv_bias,
            qkv_weight,
            proj_weight,
            proj_bias.reshape(1, channels),
        )

    return jax.shard_map(
        local,
        mesh=mesh,
        in_specs=(P("grp", "lat", None, None), P("grp")) + (P(),) * 10,
        out_specs=P("grp", "lat", None, None),
        check_vma=False,
    )
```
